512 devices in a mesh: atom: 64 (over z_hi, x, y, core), kvec: 8 (over z_lo).
Axes of the slice: x: 4, y: 4, z: 16 (z_hi: 2, z_lo: 8; z = z_hi * 8 + z_lo), core: 2. Of those that a mesh axis runs over, the one named last changes fastest.
Arguments:
- atom_coordinates: float32 [3, 131072], P(None, 'atom'), may hold values from 0 to 140
- hidden_atom_loads: float32 [8, 131072], P(None, 'atom'), may hold values from -6 to 6
- lattice_dual_points: float32 [3, 8192], P(None, 'kvec'), may hold values from -2 to 2
- screened_dual_factors: float32 [8192], P('kvec'), as said below
- loss_slope_per_lane: float32 [8], replicated, may hold values from 0.25 to 1.75
Outputs:
- charge_grad: float32 [8, 131072], P(None, ('atom', 'kvec'))
- forces: float32 [3, 131072], P(None, ('atom', 'kvec'))
- energy: float32 [8], replicated
The draws below stay inside these ranges and needn't reach their ends.
Inputs may be any that keep to these rules, and one draw needn't show every extreme that they name: `screened_dual_factors`: positive.
All inputs are finite; a program needn't handle non-finite values.
Results may differ from the reference program's by a relative error of at most 0.0003.
Values sent between devices are 32-bit elements; how exact they have to be, the bound alone decides.
No kernel may reach another device: no remote copies, remote signals or barrier semaphores. Data moves between devices by JAX's collectives and lax.ppermute only.
A program may use at most 64 MiB of HBM per device.

```python
import math
import jax
import jax.numpy as jnp
from jax import lax

C = 8
ATOMS = 131072
TOTAL_KSPACE_NUM = 8192


def draw_screened_dual_factors(key, part):
    key = jax.random.fold_in(key, 7)
    place = jnp.arange(TOTAL_KSPACE_NUM, dtype=jnp.float32) / TOTAL_KSPACE_NUM
    noise = jax.random.uniform(key, (TOTAL_KSPACE_NUM,), jnp.float32, -0.7, 0.7)
    fall = 1.2
    return jnp.exp(noise - fall * place) * (ATOMS * TOTAL_KSPACE_NUM) ** (-0.5)


def shard_levels(stream_key, extent, split, least, largest):
    loudness = 1.0
    for axis_at, parts in split:
        steps = jax.random.uniform(jax.random.fold_in(jax.random.fold_in(stream_key, 6), axis_at), (parts,), jnp.float32, least / len(split), largest / len(split))
        loudness = loudness * jnp.repeat(jnp.exp(steps), extent[axis_at] // parts).reshape((-1,) + (1,) * (len(extent) - 1 - axis_at))
    return loudness


def centred(stream_key, extent, width, limit, shards=(), kind=jnp.bfloat16):
    result = jax.random.normal(stream_key, extent, jnp.float32) * width
    if len(shards) > 0:
        result = shard_levels(stream_key, extent, shards, -0.22, 0.18) * result
    return jnp.clip(result, min=-limit, max=limit).astype(kind)


def setup_inputs(seed: int = 0) -> dict:
    seeds = jax.random.split(jax.random.key(seed), 6)
    atom_coordinates = jnp.clip(140.0 * jax.random.uniform(seeds[0], (3, ATOMS), jnp.float32) ** shard_levels(seeds[0], (3, ATOMS), ((1, 64),), -0.2, 0.2), 0.0, 140.0)
    hidden_atom_loads = centred(seeds[1], (C, ATOMS), 1.0, 6.0, ((1, 64),), jnp.float32)
    lattice_dual_points = jnp.clip(jax.random.uniform(seeds[2], (3, TOTAL_KSPACE_NUM), jnp.float32, -2.0, 2.0) * shard_levels(seeds[2], (3, TOTAL_KSPACE_NUM), ((1, 8),), -0.4, 0.0), -2.0, 2.0)
    screened_dual_factors = draw_screened_dual_factors(jax.random.fold_in(seeds[5], 71), 0)
    loss_slope_per_lane = jnp.clip(1.0 + 0.15 * jax.random.normal(seeds[4], (C,), jnp.float32), 0.25, 1.75)
    return {"atom_coordinates": atom_coordinates, "hidden_atom_loads": hidden_atom_loads, "lattice_dual_points": lattice_dual_points, "screened_dual_factors": screened_dual_factors, "loss_slope_per_lane": loss_slope_per_lane}


HIGHEST = lax.Precision.HIGHEST


def phase_angles(kspace_tile, pos):
    theta = kspace_tile[0][:, None] * pos[0][None, :] + kspace_tile[1][:, None] * pos[1][None, :]
    theta = theta + kspace_tile[2][:, None] * pos[2][None, :]
    return jnp.cos(theta), jnp.sin(theta)


def reference(atom_coordinates, hidden_atom_loads, lattice_dual_points, screened_dual_factors, loss_slope_per_lane):
    dual_point_tile = math.gcd(TOTAL_KSPACE_NUM, 128)
    tile_number = TOTAL_KSPACE_NUM // dual_point_tile
    kspace_tiles_list = lattice_dual_points.reshape(3, tile_number, dual_point_tile).transpose(1, 0, 2)
    w_blocks = screened_dual_factors.reshape(tile_number, dual_point_tile)

    def structure(kspace_tile):
        cosine_terms, sine_terms = phase_angles(kspace_tile, atom_coordinates)
        real_part = jnp.einsum("cn,kn->ck", hidden_atom_loads, cosine_terms, precision=HIGHEST)
        imag_part = jnp.einsum("cn,kn->ck", hidden_atom_loads, sine_terms, precision=HIGHEST)
        return jnp.stack([real_part, imag_part])

    factors = lax.map(structure, kspace_tiles_list)
    energy = jnp.sum(jnp.sum(w_blocks[:, None, :] * (factors[:, 0] * factors[:, 0] + factors[:, 1] * factors[:, 1]), axis=2), axis=0) / ATOMS
    coefs = 2.0 * loss_slope_per_lane[None, None, :, None] * w_blocks[:, None, None, :] * factors

    def accumulate(carry, item):
        kspace_tile, coef = item
        cosine_terms, sine_terms = phase_angles(kspace_tile, atom_coordinates)
        grad_q = carry[0] + jnp.einsum("ck,kn->cn", coef[0], cosine_terms, precision=HIGHEST) + jnp.einsum("ck,kn->cn", coef[1], sine_terms, precision=HIGHEST)
        along_real = jnp.einsum("ck,cn->kn", coef[0], hidden_atom_loads, precision=HIGHEST)
        along_imag = jnp.einsum("ck,cn->kn", coef[1], hidden_atom_loads, precision=HIGHEST)
        dtheta = along_imag * cosine_terms - along_real * sine_terms
        force = carry[1] - jnp.einsum("dk,kn->dn", kspace_tile, dtheta, precision=HIGHEST)
        return (grad_q, force), None

    init = (jnp.zeros((C, ATOMS), jnp.float32), jnp.zeros((3, ATOMS), jnp.float32))
    (charge_grad, forces), _ = lax.scan(accumulate, init, (kspace_tiles_list, coefs))
    return charge_grad, forces, energy
```

```python
import functools

import jax
import jax.numpy as jnp
import numpy as np
from jax import lax
from jax.experimental import pallas as pl
from jax.experimental.pallas import tpu as pltpu
from jax.sharding import Mesh
from jax.sharding import PartitionSpec as P

BF16 = jnp.bfloat16
F32 = jnp.float32
PLANE = ("x", "y", "c")
COLUMN = ("zh", "k")
CENTRE = 70.0
SINE = (4.442867755889893, -7.307443618774414, 3.594788074493408, -0.7843739986419678)
COSINE = (1.4142041206359863, -6.977642059326172, 5.715238571166992, -1.7283486127853394)


def halves(value):
    high = value.astype(BF16)
    return high, (value - high.astype(F32)).astype(BF16)


def pieces(value):
    first = value.astype(BF16)
    rest = value - first.astype(F32)
    second = rest.astype(BF16)
    return first, second, (rest - second.astype(F32)).astype(BF16)


def spread(value, outer):
    a, b, c = pieces(value)
    rows = [a, a, a, b, b, b, c, c, c] if outer else [a, b, c] * 3
    return jnp.concatenate(rows + [jnp.zeros((5, value.shape[1]), BF16)], axis=0)


def rows_by_rows(a, b):
    return lax.dot_general(a, b, (((0,), (0,)), ((), ())), preferred_element_type=F32)


def product(a, b):
    return lax.dot_general(a, b, (((1,), (0,)), ((), ())), preferred_element_type=F32)


def polynomial(z, terms):
    total = terms[-1]
    for term in terms[-2::-1]:
        total = term + z * total
    return total


def versine_and_sine(turns):
    g = turns - jnp.round(turns)
    z = g * g
    s = g * polynomial(z, SINE)
    c = polynomial(z, COSINE)
    return s * s, s * c


def structure_kernel(pos_ref, load_ref, dual_ref, out_ref, p_ref, q_ref, w_ref, *, bm, bn):
    atoms, vectors = pos_ref.shape[1], dual_ref.shape[1]
    p_ref[...] = spread(pos_ref[...] - CENTRE, True)
    q_ref[...] = spread(dual_ref[...] * (0.5 / np.pi), False)
    load = load_ref[...]
    w_ref[...] = jnp.concatenate(halves(load), axis=0)
    total = jnp.sum(load, axis=1, keepdims=True)
    for j in range(vectors // bn):
        q = q_ref[:, j * bn : (j + 1) * bn]
        by_versine = jnp.zeros((16, bn), F32)
        by_sine = jnp.zeros((16, bn), F32)
        for i in range(atoms // bm):
            versine, sine = versine_and_sine(rows_by_rows(p_ref[:, i * bm : (i + 1) * bm], q))
            w = w_ref[:, i * bm : (i + 1) * bm]
            for part in halves(versine):
                by_versine = by_versine + product(w, part)
            for part in halves(sine):
                by_sine = by_sine + product(w, part)
        real = total - (by_versine[:8] + by_versine[8:])
        imag = by_sine[:8] + by_sine[8:]
        factors = jnp.concatenate([real, imag], axis=0)
        for t in range(bn // 128):
            out_ref[pl.ds((j * bn + t * 128) // 8, 16), :] = factors[:, t * 128 : (t + 1) * 128]


def structure(pos, load, dual):
    atoms, vectors = pos.shape[1], dual.shape[1]
    return pl.pallas_call(
        functools.partial(structure_kernel, bm=512, bn=256),
        out_shape=jax.ShapeDtypeStruct((vectors // 8, 128), F32),
        in_specs=[pl.BlockSpec(memory_space=pltpu.VMEM)] * 3,
        out_specs=pl.BlockSpec(memory_space=pltpu.VMEM),
        scratch_shapes=[
            pltpu.VMEM((32, atoms), BF16),
            pltpu.VMEM((32, vectors), BF16),
            pltpu.VMEM((16, atoms), BF16),
        ],
        compiler_params=pltpu.CompilerParams(vmem_limit_bytes=40 * 2**20),
        name="structure",
    )(pos, load, dual)


def gradient_kernel(
    table_ref, pos_ref, load_ref, slope_ref, grad_ref, force_ref, energy_ref, p_ref, versine_ref, sine_ref, *, all_atoms, bm
):
    owned = pos_ref.shape[1]
    vectors = p_ref.shape[1]
    q = spread(pos_ref[...] - CENTRE, False)
    load = load_ref[...]
    slope = 2.0 * slope_ref[...]
    energy = jnp.zeros((8, 128), F32)
    constant = jnp.zeros((32, 128), F32)
    for g in range(vectors // 1024):
        for zl in range(8):
            rows = [
                table_ref[pl.ds((g * 4 + part) * 40 + zl, 4, stride=8), :] for part in range(4)
            ]
            dual = table_ref[pl.ds(g * 160 + 32 + zl, 4, stride=40), :]
            real = jnp.concatenate(rows[:2], axis=0)
            imag = jnp.concatenate(rows[2:], axis=0)
            weight = dual[3:4]
            energy = energy + weight * (real * real + imag * imag)
            real = slope * (weight * real)
            imag = slope * (weight * imag)
            at_cosine = jnp.concatenate([-real] + [dual[d : d + 1] * imag for d in range(3)], axis=0)
            at_sine = jnp.concatenate([imag] + [dual[d : d + 1] * real for d in range(3)], axis=0)
            constant = constant - at_cosine
            at = pl.ds((g * 8 + zl) * 128, 128)
            versine_ref[:, at] = jnp.concatenate(halves(at_cosine), axis=0)
            sine_ref[:, at] = jnp.concatenate(halves(at_sine), axis=0)
            p_ref[:, at] = spread(dual[:3] * (0.5 / np.pi), True)
    energy_ref[...] = jnp.sum(energy, axis=1, keepdims=True) * (1.0 / all_atoms)
    total = jnp.zeros((64, owned), F32)
    rest = jnp.zeros((32, owned), F32)
    for i in range(vectors // bm):
        at = slice(i * bm, (i + 1) * bm)
        versine, sine = versine_and_sine(rows_by_rows(p_ref[:, at], q))
        for value, ref in ((versine, versine_ref), (sine, sine_ref)):
            high, low = halves(value)
            total = total + product(ref[:, at], high)
            rest = rest + product(ref[:32, at], low)
    out = total[:32] + total[32:] + rest + jnp.sum(constant, axis=1, keepdims=True)
    grad_ref[...] = out[:8]
    force_ref[...] = jnp.concatenate(
        [jnp.sum(load * out[8 * d + 8 : 8 * d + 16], axis=0, keepdims=True) for d in range(3)], axis=0
    )


def gradients(table, pos, load, slope, vectors, all_atoms):
    owned = pos.shape[1]
    return pl.pallas_call(
        functools.partial(gradient_kernel, all_atoms=all_atoms, bm=512),
        out_shape=(
            jax.ShapeDtypeStruct((8, owned), F32),
            jax.ShapeDtypeStruct((3, owned), F32),
            jax.ShapeDtypeStruct((8, 1), F32),
        ),
        in_specs=[pl.BlockSpec(memory_space=pltpu.VMEM)] * 4,
        out_specs=(pl.BlockSpec(memory_space=pltpu.VMEM),) * 3,
        scratch_shapes=[
            pltpu.VMEM((32, vectors), BF16),
            pltpu.VMEM((64, vectors), BF16),
            pltpu.VMEM((64, vectors), BF16),
        ],
        compiler_params=pltpu.CompilerParams(vmem_limit_bytes=40 * 2**20),
        name="gradients",
    )(table, pos, load, slope)


def shards(pos, load, dual, weights, slope):
    owned = pos.shape[1] // lax.axis_size("k")
    mine = lax.axis_index("k") * owned
    own_pos = lax.dynamic_slice_in_dim(pos, mine, owned, 1)
    own_load = lax.dynamic_slice_in_dim(load, mine, owned, 1)
    place = lax.axis_index(PLANE)
    vectors_here = jnp.concatenate([dual, weights[None]], axis=0)
    own_vectors = lax.dynamic_slice(vectors_here, (place % 4, (place // 4) * 128), (1, 128))

    partial = structure(pos, load, dual)
    parts = lax.all_to_all(partial.reshape(32, 4, 128), PLANE, 0, 0, tiled=True)
    block = jnp.concatenate([jnp.sum(parts, axis=0), own_vectors], axis=0)
    column = lax.all_to_all(jnp.broadcast_to(block.reshape(640), (16, 640)), COLUMN, 0, 0, tiled=True)
    column = column.reshape(2, 8, 5, 128)
    block = jnp.concatenate([column[0, :, :4] + column[1, :, :4], column[0, :, 4:]], axis=1)
    block = jnp.transpose(block, (1, 0, 2)).reshape(5120)
    table = lax.all_to_all(jnp.broadcast_to(block, (32, 5120)), PLANE, 0, 0, tiled=True)
    vectors = dual.shape[1] * lax.axis_size("k")
    all_atoms = pos.shape[1] * lax.axis_size(("zh",) + PLANE)
    grad, force, energy = gradients(
        table.reshape(1280, 128), own_pos, own_load, slope.reshape(8, 1), vectors, all_atoms
    )
    return grad, force, energy.reshape(8)


def solution(mesh):
    fine = Mesh(np.asarray(mesh.devices).reshape(2, 4, 4, 2, 8), ("zh",) + PLANE + ("k",))
    atom = ("zh",) + PLANE
    return jax.shard_map(
        shards,
        mesh=fine,
        in_specs=(P(None, atom), P(None, atom), P(None, "k"), P("k"), P()),
        out_specs=(P(None, atom + ("k",)), P(None, atom + ("k",)), P()),
        check_vma=False,
    )
```

```python
import functools

import jax
import jax.numpy as jnp
import numpy as np
from jax import lax
from jax.experimental import pallas as pl
from jax.experimental.pallas import tpu as pltpu
from jax.sharding import Mesh
from jax.sharding import PartitionSpec as P

BF16 = jnp.bfloat16
F32 = jnp.float32
PLANE = ("x", "y", "c")
COLUMN = ("zh", "k")
CENTRE = 70.0
SINE = (2.2214303016662598, -0.9131746292114258, 0.10983827710151672)


def halves(value):
    high = value.astype(BF16)
    return high, (value - high.astype(F32)).astype(BF16)


def pieces(value):
    first = value.astype(BF16)
    rest = value - first.astype(F32)
    second = rest.astype(BF16)
    return first, second, (rest - second.astype(F32)).astype(BF16)


def spread(value, outer):
    a, b, c = pieces(value)
    rows = [a, a, a, b, b, b, c, c, c] if outer else [a, b, c] * 3
    return jnp.concatenate(rows + [jnp.zeros((5, value.shape[1]), BF16)], axis=0)


def rows_by_rows(a, b):
    return lax.dot_general(a, b, (((0,), (0,)), ((), ())), preferred_element_type=F32)


def product(a, b):
    return lax.dot_general(a, b, (((1,), (0,)), ((), ())), preferred_element_type=F32)


def polynomial(z, terms):
    total = terms[-1]
    for term in terms[-2::-1]:
        total = term + z * total
    return total


def versine_and_sine(turns):
    g = turns - jnp.round(turns)
    s = g * polynomial(g * g, SINE)
    versine = s * s
    square = 2.0 - versine
    sine = s * (square * lax.rsqrt(square))
    return sine * sine, sine * (1.0 - versine)


def pipelined(tiles, phase, trig_weights, turns_ref, trig_ref, step):
    rows = turns_ref.shape[1]

    def elementwise(t):
        for r in range(0, rows, step):
            versine, sine = versine_and_sine(turns_ref[t % 2, r : r + step, :])
            for part, value in enumerate(halves(versine) + halves(sine)):
                trig_ref[t % 2, part, r : r + step, :] = value

    turns_ref[0] = phase(0)
    for t in range(tiles):
        if t + 1 < tiles:
            turns_ref[(t + 1) % 2] = phase(t + 1)
        if t > 0:
            trig_weights(t - 1)
        elementwise(t)
    trig_weights(tiles - 1)


def structure_kernel(
    pos_hbm, load_hbm, dual_hbm, out_ref, pos_ref, load_ref, dual_ref, p_ref, q_ref, w_ref, turns_ref, trig_ref, sems
):
    copies = [
        pltpu.make_async_copy(source, target, sems.at[n])
        for n, (source, target) in enumerate(
            ((dual_hbm, dual_ref), (pos_hbm, pos_ref), (load_hbm, load_ref))
        )
    ]
    for copy in copies:
        copy.start()
    atoms, vectors = pos_ref.shape[1], dual_ref.shape[1]
    bm, bn = turns_ref.shape[1:]
    copies[0].wait()
    q_ref[...] = spread(dual_ref[...] * (0.5 / np.pi), False)
    copies[1].wait()
    p_ref[...] = spread(pos_ref[...] - CENTRE, True)
    copies[2].wait()
    load = load_ref[...]
    w_ref[...] = jnp.concatenate(halves(load), axis=0)
    total = jnp.sum(load, axis=1, keepdims=True)
    tiles = [(i, j) for j in range(vectors // bn) for i in range(atoms // bm)]
    sums = {}

    def phase(t):
        i, j = tiles[t]
        return rows_by_rows(p_ref[:, i * bm : (i + 1) * bm], q_ref[:, j * bn : (j + 1) * bn])

    def weigh(t):
        i, j = tiles[t]
        w = w_ref[:, i * bm : (i + 1) * bm]
        for part in range(4):
            term = product(w, trig_ref[t % 2, part])
            sums[part // 2] = sums[part // 2] + term if part % 2 or i > 0 else term
        if i == atoms // bm - 1:
            real = total - 2.0 * (sums[0][:8] + sums[0][8:])
            imag = 2.0 * (sums[1][:8] + sums[1][8:])
            factors = jnp.concatenate([real, imag], axis=0)
            for lane in range(0, bn, 128):
                out_ref[pl.ds((j * bn + lane) // 8, 16), :] = factors[:, lane : lane + 128]

    pipelined(len(tiles), phase, weigh, turns_ref, trig_ref, 16)


def structure(pos, load, dual):
    atoms, vectors = pos.shape[1], dual.shape[1]
    bm, bn = 512, 256
    return pl.pallas_call(
        structure_kernel,
        out_shape=jax.ShapeDtypeStruct((vectors // 8, 128), F32),
        in_specs=[pl.BlockSpec(memory_space=pl.ANY)] * 3,
        out_specs=pl.BlockSpec(memory_space=pltpu.VMEM),
        scratch_shapes=[
            pltpu.VMEM(pos.shape, F32),
            pltpu.VMEM(load.shape, F32),
            pltpu.VMEM(dual.shape, F32),
            pltpu.VMEM((32, atoms), BF16),
            pltpu.VMEM((32, vectors), BF16),
            pltpu.VMEM((16, atoms), BF16),
            pltpu.VMEM((2, bm, bn), F32),
            pltpu.VMEM((2, 4, bm, bn), BF16),
            pltpu.SemaphoreType.DMA((3,)),
        ],
        compiler_params=pltpu.CompilerParams(vmem_limit_bytes=60 * 2**20),
        name="structure",
    )(pos, load, dual)


def gradient_kernel(
    table_ref,
    pos_ref,
    load_ref,
    slope_ref,
    grad_ref,
    force_ref,
    energy_ref,
    p_ref,
    versine_ref,
    sine_ref,
    turns_ref,
    trig_ref,
    *,
    all_atoms,
):
    bm, owned = turns_ref.shape[1:]
    vectors = p_ref.shape[1]
    q = spread(pos_ref[...] - CENTRE, False)
    load = load_ref[...]
    slope = 2.0 * slope_ref[...]
    sums = {
        "energy": jnp.zeros((8, 128), F32),
        "constant": jnp.zeros((32, 128), F32),
        "high": jnp.zeros((64, owned), F32),
        "low": jnp.zeros((32, owned), F32),
    }

    def duals(b):
        return table_ref[pl.ds((b // 8) * 160 + 32 + b % 8, 4, stride=40), :]

    def weights(b):
        g, zl = b // 8, b % 8
        rows = [table_ref[pl.ds((g * 4 + part) * 40 + zl, 4, stride=8), :] for part in range(4)]
        dual = duals(b)
        real = jnp.concatenate(rows[:2], axis=0)
        imag = jnp.concatenate(rows[2:], axis=0)
        weight = dual[3:4]
        sums["energy"] = sums["energy"] + weight * (real * real + imag * imag)
        real = slope * (weight * real)
        imag = slope * (weight * imag)
        at_cosine = jnp.concatenate([real] + [-dual[d : d + 1] * imag for d in range(3)], axis=0)
        at_sine = jnp.concatenate([imag] + [dual[d : d + 1] * real for d in range(3)], axis=0)
        sums["constant"] = sums["constant"] + at_cosine
        at = pl.ds(b * 128, 128)
        versine_ref[:, at] = jnp.concatenate(halves(-2.0 * at_cosine), axis=0)
        sine_ref[:, at] = jnp.concatenate(halves(2.0 * at_sine), axis=0)

    def phase(t):
        at = slice(t * bm, (t + 1) * bm)
        for b in range(t * bm // 128, (t + 1) * bm // 128):
            p_ref[:, b * 128 : (b + 1) * 128] = spread(duals(b)[:3] * (0.5 / np.pi), True)
        return rows_by_rows(p_ref[:, at], q)

    def weigh(t):
        at = slice(t * bm, (t + 1) * bm)
        for b in range(t * bm // 128, (t + 1) * bm // 128):
            weights(b)
        for part, ref in enumerate((versine_ref, sine_ref)):
            sums["high"] = sums["high"] + product(ref[:, at], trig_ref[t % 2, 2 * part])
            sums["low"] = sums["low"] + product(ref[:32, at], trig_ref[t % 2, 2 * part + 1])

    pipelined(vectors // bm, phase, weigh, turns_ref, trig_ref, 16)
    energy = jnp.sum(sums["energy"], axis=1, keepdims=True) * (1.0 / all_atoms)
    eye = lax.broadcasted_iota(jnp.int32, (8, 8), 0) == lax.broadcasted_iota(jnp.int32, (8, 8), 1)
    energy_ref[...] = jnp.sum(jnp.where(eye, energy, 0.0), axis=0, keepdims=True)
    out = sums["high"][:32] + sums["high"][32:] + sums["low"]
    out = out + jnp.sum(sums["constant"], axis=1, keepdims=True)
    grad_ref[...] = out[:8]
    force_ref[...] = jnp.concatenate(
        [jnp.sum(load * out[8 * d + 8 : 8 * d + 16], axis=0, keepdims=True) for d in range(3)], axis=0
    )


def gradients(table, pos, load, slope, vectors, all_atoms):
    owned = pos.shape[1]
    bm = 512
    return pl.pallas_call(
        functools.partial(gradient_kernel, all_atoms=all_atoms),
        out_shape=(
            jax.ShapeDtypeStruct((8, owned), F32),
            jax.ShapeDtypeStruct((3, owned), F32),
            jax.ShapeDtypeStruct((1, 8), F32),
        ),
        in_specs=[pl.BlockSpec(memory_space=pltpu.VMEM)] * 4,
        out_specs=(pl.BlockSpec(memory_space=pltpu.VMEM),) * 3,
        scratch_shapes=[
            pltpu.VMEM((32, vectors), BF16),
            pltpu.VMEM((64, vectors), BF16),
            pltpu.VMEM((64, vectors), BF16),
            pltpu.VMEM((2, bm, owned), F32),
            pltpu.VMEM((2, 4, bm, owned), BF16),
        ],
        compiler_params=pltpu.CompilerParams(vmem_limit_bytes=40 * 2**20),
        name="gradients",
    )(table, pos, load, slope)


def shards(pos, load, dual, weights, slope):
    owned = pos.shape[1] // lax.axis_size("k")
    mine = lax.axis_index("k") * owned
    own_pos = lax.dynamic_slice_in_dim(pos, mine, owned, 1)
    own_load = lax.dynamic_slice_in_dim(load, mine, owned, 1)
    place = lax.axis_index(PLANE)
    vectors_here = jnp.concatenate([dual, weights[None]], axis=0)
    own_vectors = lax.dynamic_slice(vectors_here, (place % 4, (place // 4) * 128), (1, 128))

    partial = structure(pos, load, dual)
    parts = lax.all_to_all(partial.reshape(32, 4, 128), PLANE, 0, 0, tiled=True)
    block = jnp.concatenate([jnp.sum(parts, axis=0), own_vectors], axis=0)
    column = lax.all_to_all(jnp.broadcast_to(block.reshape(640), (16, 640)), COLUMN, 0, 0, tiled=True)
    column = column.reshape(2, 8, 5, 128)
    block = jnp.concatenate([column[0, :, :4] + column[1, :, :4], column[0, :, 4:]], axis=1)
    block = jnp.transpose(block, (1, 0, 2)).reshape(40, 128)
    table = lax.all_to_all(jnp.broadcast_to(block, (32, 40, 128)), PLANE, 0, 0, tiled=True)
    vectors = dual.shape[1] * lax.axis_size("k")
    all_atoms = pos.shape[1] * lax.axis_size(("zh",) + PLANE)
    grad, force, energy = gradients(
        table.reshape(1280, 128), own_pos, own_load, slope.reshape(8, 1), vectors, all_atoms
    )
    return grad, force, energy.reshape(8)


def solution(mesh):
    fine = Mesh(np.asarray(mesh.devices).reshape(2, 4, 4, 2, 8), ("zh",) + PLANE + ("k",))
    atom = ("zh",) + PLANE
    return jax.shard_map(
        shards,
        mesh=fine,
        in_specs=(P(None, atom), P(None, atom), P(None, "k"), P("k"), P()),
        out_specs=(P(None, atom + ("k",)), P(None, atom + ("k",)), P()),
        check_vma=False,
    )
```

```python
import functools

import jax
import jax.numpy as jnp
import numpy as np
from jax import lax
from jax.experimental import pallas as pl
from jax.experimental.pallas import tpu as pltpu
from jax.sharding import Mesh
from jax.sharding import PartitionSpec as P

BF16 = jnp.bfloat16
F32 = jnp.float32
PLANE = ("x", "y", "c")
COLUMN = ("zh", "k")
PLANE_FLIP = 20
CORE_PLANE_FLIP = 10
COLUMN_ORDER = (*range(8, 16), *range(8))
CENTRE = 70.0
SINE = (2.2214303016662598, -0.9131746292114258, 0.10983827710151672)


def halves(value):
    high = value.astype(BF16)
    return high, (value - high.astype(F32)).astype(BF16)


def pieces(value):
    first = value.astype(BF16)
    rest = value - first.astype(F32)
    second = rest.astype(BF16)
    return first, second, (rest - second.astype(F32)).astype(BF16)


def spread(value, outer):
    a, b, c = pieces(value)
    rows = [a, a, a, b, b, b, c, c, c] if outer else [a, b, c] * 3
    return jnp.concatenate(rows + [jnp.zeros((5, value.shape[1]), BF16)], axis=0)


def rows_by_rows(a, b):
    return lax.dot_general(a, b, (((0,), (0,)), ((), ())), preferred_element_type=F32)


def product(a, b):
    return lax.dot_general(a, b, (((1,), (0,)), ((), ())), preferred_element_type=F32)


def polynomial(z, terms):
    total = terms[-1]
    for term in terms[-2::-1]:
        total = term + z * total
    return total


def versine_and_sine(turns):
    g = turns - jnp.round(turns)
    s = g * polynomial(g * g, SINE)
    versine = s * s
    square = 2.0 - versine
    sine = s * (square * lax.rsqrt(square))
    return sine * sine, sine * (1.0 - versine)


def pipelined(tiles, phase, trig_weights, turns_ref, trig_ref, step):
    rows = turns_ref.shape[1]

    def elementwise(t):
        for r in range(0, rows, step):
            versine, sine = versine_and_sine(turns_ref[t % 2, r : r + step, :])
            for part, value in enumerate(halves(versine) + halves(sine)):
                trig_ref[t % 2, part, r : r + step, :] = value

    turns_ref[0] = phase(0)
    for t in range(tiles):
        if t + 1 < tiles:
            turns_ref[(t + 1) % 2] = phase(t + 1)
        if t > 0:
            trig_weights(t - 1)
        elementwise(t)
    trig_weights(tiles - 1)


def structure_kernel(
    pos_hbm, load_hbm, dual_hbm, out_ref, pos_ref, load_ref, dual_ref, p_ref, q_ref, w_ref, turns_ref, trig_ref, sems
):
    copies = [
        pltpu.make_async_copy(source, target, sems.at[n])
        for n, (source, target) in enumerate(
            ((dual_hbm, dual_ref), (pos_hbm, pos_ref), (load_hbm, load_ref))
        )
    ]
    for copy in copies:
        copy.start()
    atoms, vectors = pos_ref.shape[1], dual_ref.shape[1]
    bm, bn = turns_ref.shape[1:]
    copies[0].wait()
    q_ref[...] = spread(dual_ref[...] * (0.5 / np.pi), False)
    copies[1].wait()
    p_ref[...] = spread(pos_ref[...] - CENTRE, True)
    copies[2].wait()
    load = load_ref[...]
    w_ref[...] = jnp.concatenate(halves(load), axis=0)
    total = jnp.sum(load, axis=1, keepdims=True)
    tiles = [(i, j) for j in range(vectors // bn) for i in range(atoms // bm)]
    sums = {}

    def phase(t):
        i, j = tiles[t]
        return rows_by_rows(p_ref[:, i * bm : (i + 1) * bm], q_ref[:, j * bn : (j + 1) * bn])

    def weigh(t):
        i, j = tiles[t]
        w = w_ref[:, i * bm : (i + 1) * bm]
        for part in range(4):
            term = product(w, trig_ref[t % 2, part])
            sums[part // 2] = sums[part // 2] + term if part % 2 or i > 0 else term
        if i == atoms // bm - 1:
            real = total - 2.0 * (sums[0][:8] + sums[0][8:])
            imag = 2.0 * (sums[1][:8] + sums[1][8:])
            factors = jnp.concatenate([real, imag], axis=0)
            for lane in range(0, bn, 128):
                group = (j * bn + lane) // 128
                for part in range(4):
                    place = ((group % 4) * 8 + part * 2 + group // 4) ^ PLANE_FLIP
                    out_ref[place * 4 : place * 4 + 4, :] = factors[
                        part * 4 : part * 4 + 4, lane : lane + 128
                    ]

    pipelined(len(tiles), phase, weigh, turns_ref, trig_ref, 16)


def structure(pos, load, dual):
    atoms, vectors = pos.shape[1], dual.shape[1]
    bm, bn = 512, 256
    return pl.pallas_call(
        structure_kernel,
        out_shape=jax.ShapeDtypeStruct((vectors // 8, 128), F32),
        in_specs=[pl.BlockSpec(memory_space=pl.ANY)] * 3,
        out_specs=pl.BlockSpec(memory_space=pltpu.VMEM),
        scratch_shapes=[
            pltpu.VMEM(pos.shape, F32),
            pltpu.VMEM(load.shape, F32),
            pltpu.VMEM(dual.shape, F32),
            pltpu.VMEM((32, atoms), BF16),
            pltpu.VMEM((32, vectors), BF16),
            pltpu.VMEM((16, atoms), BF16),
            pltpu.VMEM((2, bm, bn), F32),
            pltpu.VMEM((2, 4, bm, bn), BF16),
            pltpu.SemaphoreType.DMA((3,)),
        ],
        compiler_params=pltpu.CompilerParams(vmem_limit_bytes=60 * 2**20),
        name="structure",
    )(pos, load, dual)


def spread_four(value, outer):
    twice = jnp.concatenate([value, value], axis=0)
    a = twice.astype(BF16).astype(F32)
    rest = twice - a
    b = rest.astype(BF16).astype(F32)
    c = rest - b
    first = lax.broadcasted_iota(jnp.int32, twice.shape, 0) < 4
    if outer:
        rows = [a, jnp.where(first, a, b), b, c]
    else:
        rows = [jnp.where(first, a, b), jnp.where(first, c, a), jnp.where(first, b, c), jnp.where(first, a, b)]
    return jnp.concatenate(rows, axis=0).astype(BF16)


def gradient_kernel(
    table_ref,
    atoms_ref,
    slope_ref,
    out_ref,
    p_ref,
    versine_ref,
    sine_ref,
    turns_ref,
    trig_ref,
    *,
    all_atoms,
):
    bm, owned = turns_ref.shape[1:]
    vectors = p_ref.shape[1]
    atoms = jnp.concatenate([atoms_ref[0], atoms_ref[1]], axis=1)
    load = atoms[:8]
    pos = jnp.concatenate([atoms[8:11] - CENTRE, jnp.zeros((1, owned), F32)], axis=0)
    q = spread_four(pos, False)
    slope = 4.0 * slope_ref[...]
    is_dual = lax.broadcasted_iota(jnp.int32, (4, 128), 0) < 3
    sums = {
        "energy": jnp.zeros((8, 128), F32),
        "constant": jnp.zeros((32, 128), F32),
        "high": jnp.zeros((64, owned), F32),
        "low": jnp.zeros((32, owned), F32),
    }

    def duals(b):
        places = [((b // 8) * 4 + part) ^ CORE_PLANE_FLIP for part in range(4)]
        return jnp.concatenate([table_ref[pl.ds(at * 40 + 32 + b % 8, 1), :] for at in places], axis=0)

    def weights(b):
        g, zl = b // 8, b % 8
        rows = [
            table_ref[pl.ds(((g * 4 + part) ^ CORE_PLANE_FLIP) * 40 + zl, 4, stride=8), :]
            for part in range(4)
        ]
        dual = duals(b)
        real = jnp.concatenate(rows[:2], axis=0)
        imag = jnp.concatenate(rows[2:], axis=0)
        weight = dual[3:4]
        real_term, imag_term = weight * real, weight * imag
        sums["energy"] = sums["energy"] + (real_term * real + imag_term * imag)
        real_term, imag_term = slope * real_term, slope * imag_term
        at_versine = jnp.concatenate([-real_term] + [dual[d : d + 1] * imag_term for d in range(3)], axis=0)
        at_sine = jnp.concatenate([imag_term] + [dual[d : d + 1] * real_term for d in range(3)], axis=0)
        sums["constant"] = sums["constant"] + at_versine
        at = pl.ds(b * 128, 128)
        versine_ref[:, at] = jnp.concatenate(halves(at_versine), axis=0)
        sine_ref[:, at] = jnp.concatenate(halves(at_sine), axis=0)

    def phase(t):
        at = slice(t * bm, (t + 1) * bm)
        for b in range(t * bm // 128, (t + 1) * bm // 128):
            dual = jnp.where(is_dual, duals(b) * (0.5 / np.pi), 0.0)
            p_ref[:, b * 128 : (b + 1) * 128] = spread_four(dual, True)
        return rows_by_rows(p_ref[:, at], q)

    def weigh(t):
        at = slice(t * bm, (t + 1) * bm)
        for b in range(t * bm // 128, (t + 1) * bm // 128):
            weights(b)
        for part, ref in enumerate((versine_ref, sine_ref)):
            sums["high"] = sums["high"] + product(ref[:, at], trig_ref[t % 2, 2 * part])
            sums["low"] = sums["low"] + product(ref[:32, at], trig_ref[t % 2, 2 * part + 1])

    pipelined(vectors // bm, phase, weigh, turns_ref, trig_ref, 16)
    energy = jnp.sum(sums["energy"], axis=1, keepdims=True) * (1.0 / all_atoms)
    shape = (8, owned)
    diagonal = lax.broadcasted_iota(jnp.int32, shape, 0) == lax.broadcasted_iota(jnp.int32, shape, 1)
    out = sums["high"][:32] + sums["high"][32:] + sums["low"]
    out = out - 0.5 * jnp.sum(sums["constant"], axis=1, keepdims=True)
    out_ref[:8] = out[:8]
    out_ref[8:12] = jnp.concatenate(
        [jnp.sum(load * out[8 * d + 8 : 8 * d + 16], axis=0, keepdims=True) for d in range(3)]
        + [jnp.sum(jnp.where(diagonal, energy, 0.0), axis=0, keepdims=True)],
        axis=0,
    )


def gradients(table, atoms, slope, vectors, all_atoms):
    owned = 2 * atoms.shape[2]
    bm = 256
    return pl.pallas_call(
        functools.partial(gradient_kernel, all_atoms=all_atoms),
        out_shape=jax.ShapeDtypeStruct((12, owned), F32),
        in_specs=[pl.BlockSpec(memory_space=pltpu.VMEM)] * 3,
        out_specs=pl.BlockSpec(memory_space=pltpu.VMEM),
        scratch_shapes=[
            pltpu.VMEM((32, vectors), BF16),
            pltpu.VMEM((64, vectors), BF16),
            pltpu.VMEM((64, vectors), BF16),
            pltpu.VMEM((2, bm, owned), F32),
            pltpu.VMEM((2, 4, bm, owned), BF16),
        ],
        compiler_params=pltpu.CompilerParams(vmem_limit_bytes=40 * 2**20),
        name="gradients",
    )(table, atoms, slope)


def shards(pos, load, dual, weights, slope):
    owned = pos.shape[1] // lax.axis_size("k")
    place = lax.axis_index(PLANE)
    vectors_here = jnp.concatenate([dual, weights[None]], axis=0)
    group = (place % 2) * 4 + place // 8
    own_vectors = lax.dynamic_slice(vectors_here, (place // 2 % 4, group * 128), (1, 128))

    partial = structure(pos, load, dual)
    parts = lax.all_to_all(
        partial.reshape(32, 4, 128),
        PLANE,
        0,
        0,
        axis_index_groups=[[n ^ PLANE_FLIP for n in range(32)]],
        tiled=True,
    )
    block = jnp.concatenate([jnp.sum(parts, axis=0), own_vectors], axis=0)
    column = lax.all_to_all(
        jnp.broadcast_to(block.reshape(640), (16, 640)),
        COLUMN,
        0,
        0,
        axis_index_groups=[list(COLUMN_ORDER)],
        tiled=True,
    )
    column = column.reshape(2, 8, 5, 128)[::-1]
    block = jnp.concatenate([column[0, :, :4] + column[1, :, :4], column[0, :, 4:]], axis=1)
    block = jnp.transpose(block, (1, 0, 2)).reshape(40, 128)

    mine = lax.axis_index("k") * owned
    atoms = jnp.concatenate(
        [lax.dynamic_slice_in_dim(load, mine, owned, 1), lax.dynamic_slice_in_dim(pos, mine, owned, 1)], axis=0
    )
    atoms, slope, _ = lax.optimization_barrier((atoms, slope, column))
    atoms = lax.all_gather(atoms, "c")
    table = lax.all_to_all(
        jnp.broadcast_to(block, (16, 40, 128)),
        ("x", "y"),
        0,
        0,
        axis_index_groups=[[n ^ CORE_PLANE_FLIP for n in range(16)]],
        tiled=True,
    )
    vectors = dual.shape[1] * lax.axis_size("k") // 2
    all_atoms = pos.shape[1] * lax.axis_size(("zh",) + PLANE)
    shares = lax.all_gather(
        gradients(table.reshape(640, 128), atoms, slope.reshape(8, 1), vectors, all_atoms), "c"
    )
    sums = shares[0] + shares[1]
    result = lax.dynamic_slice_in_dim(sums, lax.axis_index("c") * owned, owned, 1)
    return result[:8], result[8:11], sums[11, :8]


def solution(mesh):
    fine = Mesh(np.asarray(mesh.devices).reshape(2, 4, 4, 2, 8), ("zh",) + PLANE + ("k",))
    atom = ("zh",) + PLANE
    return jax.shard_map(
        shards,
        mesh=fine,
        in_specs=(P(None, atom), P(None, atom), P(None, "k"), P("k"), P()),
        out_specs=(P(None, atom + ("k",)), P(None, atom + ("k",)), P()),
        check_vma=False,
    )
```

```python
import functools

import jax
import jax.numpy as jnp
import numpy as np
from jax import lax
from jax.experimental import pallas as pl
from jax.experimental.pallas import tpu as pltpu
from jax.sharding import Mesh
from jax.sharding import PartitionSpec as P

BF16 = jnp.bfloat16
F32 = jnp.float32
PLANE = ("x", "y", "c")
COLUMN = ("zh", "k")
PLANE_FLIP = 20
CORE_PLANE_FLIP = 10
COLUMN_ORDER = (*range(8, 16), *range(8))
CENTRE = 70.0
SINE = (2.2214303016662598, -0.9131746292114258, 0.10983827710151672)


def halves(value):
    high = value.astype(BF16)
    return high, (value - high.astype(F32)).astype(BF16)


def pieces(value):
    first = value.astype(BF16)
    rest = value - first.astype(F32)
    second = rest.astype(BF16)
    return first, second, (rest - second.astype(F32)).astype(BF16)


def spread(value, outer):
    a, b, c = pieces(value)
    rows = [a, a, a, b, b, b, c, c, c] if outer else [a, b, c] * 3
    return jnp.concatenate(rows + [jnp.zeros((5, value.shape[1]), BF16)], axis=0)


def rows_by_rows(a, b):
    return lax.dot_general(a, b, (((0,), (0,)), ((), ())), preferred_element_type=F32)


def product(a, b):
    return lax.dot_general(a, b, (((1,), (0,)), ((), ())), preferred_element_type=F32)


def polynomial(z, terms):
    total = terms[-1]
    for term in terms[-2::-1]:
        total = term + z * total
    return total


def versine_and_sine(turns):
    g = turns - jnp.round(turns)
    s = g * polynomial(g * g, SINE)
    versine = s * s
    square = 2.0 - versine
    sine = s * (square * lax.rsqrt(square))
    return sine * sine, sine * (1.0 - versine)


def pipelined(tiles, phase, trig_weights, turns_ref, trig_ref, step):
    rows = turns_ref.shape[1]

    def elementwise(t):
        for r in range(0, rows, step):
            versine, sine = versine_and_sine(turns_ref[t % 2, r : r + step, :])
            for part, value in enumerate(halves(versine) + halves(sine)):
                trig_ref[t % 2, part, r : r + step, :] = value

    turns_ref[0] = phase(0)
    for t in range(tiles):
        if t + 1 < tiles:
            turns_ref[(t + 1) % 2] = phase(t + 1)
        if t > 0:
            trig_weights(t - 1)
        elementwise(t)
    trig_weights(tiles - 1)


def diagonal(width):
    shape = (8, width)
    return lax.broadcasted_iota(jnp.int32, shape, 0) == lax.broadcasted_iota(jnp.int32, shape, 1)


def structure_kernel(
    pos_hbm,
    load_hbm,
    dual_hbm,
    weight_hbm,
    slope_hbm,
    out_ref,
    own_atoms_ref,
    pos_ref,
    load_ref,
    dual_ref,
    weight_ref,
    slope_ref,
    p_ref,
    q_ref,
    w_ref,
    turns_ref,
    trig_ref,
    sems,
):
    pairs = (
        (dual_hbm, dual_ref),
        (pos_hbm, pos_ref),
        (load_hbm, load_ref),
        (weight_hbm, weight_ref),
        (slope_hbm, slope_ref),
    )
    copies = [
        pltpu.make_async_copy(source, target, sems.at[n]) for n, (source, target) in enumerate(pairs)
    ]
    for copy in copies:
        copy.start()
    atoms, vectors = pos_ref.shape[1], dual_ref.shape[1]
    bm, bn = turns_ref.shape[1:]
    copies[0].wait()
    q_ref[...] = spread(dual_ref[...] * (0.5 / np.pi), False)
    copies[1].wait()
    p_ref[...] = spread(pos_ref[...] - CENTRE, True)
    copies[2].wait()
    load = load_ref[...]
    w_ref[...] = jnp.concatenate(halves(load), axis=0)
    total = jnp.sum(load, axis=1, keepdims=True)
    tiles = [(i, j) for j in range(vectors // bn) for i in range(atoms // bm)]
    sums = {}

    def phase(t):
        i, j = tiles[t]
        return rows_by_rows(p_ref[:, i * bm : (i + 1) * bm], q_ref[:, j * bn : (j + 1) * bn])

    def weigh(t):
        i, j = tiles[t]
        w = w_ref[:, i * bm : (i + 1) * bm]
        for part in range(4):
            term = product(w, trig_ref[t % 2, part])
            sums[part // 2] = sums[part // 2] + term if part % 2 or i > 0 else term
        if i == atoms // bm - 1:
            real = total - 2.0 * (sums[0][:8] + sums[0][8:])
            imag = 2.0 * (sums[1][:8] + sums[1][8:])
            factors = jnp.concatenate([real, imag], axis=0)
            for lane in range(0, bn, 128):
                group = (j * bn + lane) // 128
                for row in range(16):
                    put(group, row // 4, row % 4, factors[row : row + 1, lane : lane + 128])

    def put(group, part, row, value):
        place = ((group % 4) * 8 + part * 2 + group // 4) ^ PLANE_FLIP
        out_ref[place, :, row * 128 : (row + 1) * 128] = value

    pipelined(len(tiles), phase, weigh, turns_ref, trig_ref, 16)

    copies[3].wait()
    for group in range(vectors // 128):
        lanes = slice(group * 128, (group + 1) * 128)
        for part in range(3):
            put(group, part, 4, dual_ref[part : part + 1, lanes])
        put(group, 3, 4, weight_ref[:, lanes])
    copies[4].wait()
    owned = own_atoms_ref.shape[1]
    mine = pl.ds(pl.multiple_of(lax.axis_index("k") * owned, 128), owned)
    own_atoms_ref[:8] = load_ref[:, mine]
    slope = jnp.concatenate([slope_ref[...], jnp.zeros((1, owned - 8), F32)], axis=1)
    own_atoms_ref[8:12] = jnp.concatenate([pos_ref[:, mine], slope], axis=0)


def structure(pos, load, dual, weights, slope, owned):
    atoms, vectors = pos.shape[1], dual.shape[1]
    bm, bn = 512, 256
    return pl.pallas_call(
        structure_kernel,
        out_shape=(
            pltpu.VMEM((32, 1, 640), F32),
            pltpu.VMEM((12, owned), F32),
        ),
        in_specs=[pl.BlockSpec(memory_space=pl.ANY)] * 5,
        out_specs=(pl.BlockSpec(memory_space=pltpu.VMEM),) * 2,
        scratch_shapes=[
            pltpu.VMEM(pos.shape, F32),
            pltpu.VMEM(load.shape, F32),
            pltpu.VMEM(dual.shape, F32),
            pltpu.VMEM(weights.shape, F32),
            pltpu.VMEM(slope.shape, F32),
            pltpu.VMEM((32, atoms), BF16),
            pltpu.VMEM((32, vectors), BF16),
            pltpu.VMEM((16, atoms), BF16),
            pltpu.VMEM((2, bm, bn), F32),
            pltpu.VMEM((2, 4, bm, bn), BF16),
            pltpu.SemaphoreType.DMA((5,)),
        ],
        compiler_params=pltpu.CompilerParams(vmem_limit_bytes=60 * 2**20),
        name="structure",
    )(pos, load, dual, weights, slope)


def spread_four(value, outer):
    twice = jnp.concatenate([value, value], axis=0)
    a = twice.astype(BF16).astype(F32)
    rest = twice - a
    b = rest.astype(BF16).astype(F32)
    c = rest - b
    first = lax.broadcasted_iota(jnp.int32, twice.shape, 0) < 4
    if outer:
        rows = [a, jnp.where(first, a, b), b, c]
    else:
        rows = [jnp.where(first, a, b), jnp.where(first, c, a), jnp.where(first, b, c), jnp.where(first, a, b)]
    return jnp.concatenate(rows, axis=0).astype(BF16)


def gradient_kernel(
    table_ref,
    atoms_ref,
    out_ref,
    p_ref,
    versine_ref,
    sine_ref,
    turns_ref,
    trig_ref,
    *,
    all_atoms,
):
    bm, owned = turns_ref.shape[1:]
    vectors = p_ref.shape[1]
    atoms = jnp.concatenate([atoms_ref[0], atoms_ref[1]], axis=1)
    load = atoms[:8]
    pos = jnp.concatenate([atoms[8:11] - CENTRE, jnp.zeros((1, owned), F32)], axis=0)
    q = spread_four(pos, False)
    slope = 4.0 * jnp.sum(jnp.where(diagonal(128), atoms_ref[0, 11:12, :128], 0.0), axis=1, keepdims=True)
    is_dual = lax.broadcasted_iota(jnp.int32, (4, 128), 0) < 3
    sums = {
        "energy": jnp.zeros((8, 128), F32),
        "constant": jnp.zeros((32, 128), F32),
        "high": jnp.zeros((64, owned), F32),
        "low": jnp.zeros((32, owned), F32),
    }

    def duals(b):
        places = [((b // 8) * 4 + part) ^ CORE_PLANE_FLIP for part in range(4)]
        return jnp.concatenate([table_ref[pl.ds(at * 40 + 32 + b % 8, 1), :] for at in places], axis=0)

    def weights(b):
        g, zl = b // 8, b % 8
        rows = [
            table_ref[pl.ds(((g * 4 + part) ^ CORE_PLANE_FLIP) * 40 + zl, 4, stride=8), :]
            for part in range(4)
        ]
        dual = duals(b)
        real = jnp.concatenate(rows[:2], axis=0)
        imag = jnp.concatenate(rows[2:], axis=0)
        weight = dual[3:4]
        real_term, imag_term = weight * real, weight * imag
        sums["energy"] = sums["energy"] + (real_term * real + imag_term * imag)
        real_term, imag_term = slope * real_term, slope * imag_term
        at_versine = jnp.concatenate([-real_term] + [dual[d : d + 1] * imag_term for d in range(3)], axis=0)
        at_sine = jnp.concatenate([imag_term] + [dual[d : d + 1] * real_term for d in range(3)], axis=0)
        sums["constant"] = sums["constant"] + at_versine
        at = pl.ds(b * 128, 128)
        versine_ref[:, at] = jnp.concatenate(halves(at_versine), axis=0)
        sine_ref[:, at] = jnp.concatenate(halves(at_sine), axis=0)

    def phase(t):
        at = slice(t * bm, (t + 1) * bm)
        for b in range(t * bm // 128, (t + 1) * bm // 128):
            dual = jnp.where(is_dual, duals(b) * (0.5 / np.pi), 0.0)
            p_ref[:, b * 128 : (b + 1) * 128] = spread_four(dual, True)
        return rows_by_rows(p_ref[:, at], q)

    def weigh(t):
        at = slice(t * bm, (t + 1) * bm)
        for b in range(t * bm // 128, (t + 1) * bm // 128):
            weights(b)
        for part, ref in enumerate((versine_ref, sine_ref)):
            sums["high"] = sums["high"] + product(ref[:, at], trig_ref[t % 2, 2 * part])
            sums["low"] = sums["low"] + product(ref[:32, at], trig_ref[t % 2, 2 * part + 1])

    pipelined(vectors // bm, phase, weigh, turns_ref, trig_ref, 16)
    energy = jnp.sum(sums["energy"], axis=1, keepdims=True) * (1.0 / all_atoms)
    out = sums["high"][:32] + sums["high"][32:] + sums["low"]
    out = out - 0.5 * jnp.sum(sums["constant"], axis=1, keepdims=True)
    out_ref[:8] = out[:8]
    out_ref[8:12] = jnp.concatenate(
        [jnp.sum(load * out[8 * d + 8 : 8 * d + 16], axis=0, keepdims=True) for d in range(3)]
        + [jnp.sum(jnp.where(diagonal(owned), energy, 0.0), axis=0, keepdims=True)],
        axis=0,
    )


def gradients(table, atoms, vectors, all_atoms):
    owned = 2 * atoms.shape[2]
    bm = 256
    return pl.pallas_call(
        functools.partial(gradient_kernel, all_atoms=all_atoms),
        out_shape=pltpu.VMEM((12, owned), F32),
        in_specs=[pl.BlockSpec(memory_space=pltpu.VMEM)] * 2,
        out_specs=pl.BlockSpec(memory_space=pltpu.VMEM),
        scratch_shapes=[
            pltpu.VMEM((32, vectors), BF16),
            pltpu.VMEM((64, vectors), BF16),
            pltpu.VMEM((64, vectors), BF16),
            pltpu.VMEM((2, bm, owned), F32),
            pltpu.VMEM((2, 4, bm, owned), BF16),
        ],
        compiler_params=pltpu.CompilerParams(vmem_limit_bytes=40 * 2**20),
        name="gradients",
    )(table, atoms)


def finish_kernel(shares_ref, grad_ref, force_ref, energy_ref):
    owned = grad_ref.shape[1]
    mine = pl.ds(pl.multiple_of(lax.axis_index("c") * owned, 128), owned)
    grad_ref[...] = shares_ref[0, :8, mine] + shares_ref[1, :8, mine]
    force_ref[...] = shares_ref[0, 8:11, mine] + shares_ref[1, 8:11, mine]
    energy_ref[...] = shares_ref[0, 11:12, :8] + shares_ref[1, 11:12, :8]


def finish(shares):
    owned = shares.shape[2] // 2
    return pl.pallas_call(
        finish_kernel,
        out_shape=(
            jax.ShapeDtypeStruct((8, owned), F32),
            jax.ShapeDtypeStruct((3, owned), F32),
            jax.ShapeDtypeStruct((1, 8), F32),
        ),
        in_specs=[pl.BlockSpec(memory_space=pltpu.VMEM)],
        out_specs=(pl.BlockSpec(memory_space=pltpu.VMEM),) * 3,
        name="finish",
    )(shares)


def shards(pos, load, dual, weights, slope):
    owned = pos.shape[1] // lax.axis_size("k")
    partial, atoms = structure(
        pos, load, dual, weights.reshape(1, -1), slope.reshape(1, -1), owned
    )
    parts = lax.all_to_all(
        partial,
        PLANE,
        0,
        0,
        axis_index_groups=[[n ^ PLANE_FLIP for n in range(32)]],
        tiled=True,
    )
    block = jnp.concatenate([jnp.sum(parts[:, :, :512], axis=0), parts[0, :, 512:]], axis=1)
    atoms, block = lax.optimization_barrier((atoms, block))
    atoms = lax.all_gather(atoms, "c")
    column = lax.all_to_all(
        jnp.broadcast_to(block, (16, 1, 640)),
        COLUMN,
        0,
        0,
        axis_index_groups=[list(COLUMN_ORDER)],
        tiled=True,
    )
    atoms, column = lax.optimization_barrier((atoms, column))
    column = column.reshape(2, 8, 5, 128)
    block = jnp.concatenate([column[1, :, :4] + column[0, :, :4], column[0, :, 4:]], axis=1)
    block = jnp.transpose(block, (1, 0, 2)).reshape(40, 128)
    table = lax.all_to_all(
        jnp.broadcast_to(block, (16, 40, 128)),
        ("x", "y"),
        0,
        0,
        axis_index_groups=[[n ^ CORE_PLANE_FLIP for n in range(16)]],
        tiled=True,
    )
    vectors = dual.shape[1] * lax.axis_size("k") // 2
    all_atoms = pos.shape[1] * lax.axis_size(("zh",) + PLANE)
    shares = lax.all_gather(gradients(table.reshape(640, 128), atoms, vectors, all_atoms), "c")
    grad, force, energy = finish(shares)
    return grad, force, energy.reshape(8)


def solution(mesh):
    fine = Mesh(np.asarray(mesh.devices).reshape(2, 4, 4, 2, 8), ("zh",) + PLANE + ("k",))
    atom = ("zh",) + PLANE
    return jax.shard_map(
        shards,
        mesh=fine,
        in_specs=(P(None, atom), P(None, atom), P(None, "k"), P("k"), P()),
        out_specs=(P(None, atom + ("k",)), P(None, atom + ("k",)), P()),
        check_vma=False,
    )
```

```python
import functools

import jax
import jax.numpy as jnp
import numpy as np
from jax import lax
from jax.experimental import pallas as pl
from jax.experimental.pallas import tpu as pltpu
from jax.sharding import Mesh
from jax.sharding import PartitionSpec as P

BF16 = jnp.bfloat16
F32 = jnp.float32
PLANE = ("x", "y", "c")
COLUMN = ("zh", "k")
PLANE_ORDER = sorted(range(32), key=lambda p: (abs(p // 8 - 2) + abs(p // 2 % 4 - 2), p ^ 1))
CORE_PLANE_ORDER = sorted(range(16), key=lambda p: abs(p // 4 - 2) + abs(p % 4 - 2))
COLUMN_ORDER = (*range(8, 16), *range(8))
CENTRE = 70.0
SINE = (2.2214303016662598, -0.9131746292114258, 0.10983827710151672)


def halves(value):
    high = value.astype(BF16)
    return high, (value - high.astype(F32)).astype(BF16)


def pieces(value):
    first = value.astype(BF16)
    rest = value - first.astype(F32)
    second = rest.astype(BF16)
    return first, second, (rest - second.astype(F32)).astype(BF16)


def spread(value, outer):
    a, b, c = pieces(value)
    rows = [a, a, a, b, b, b, c, c, c] if outer else [a, b, c] * 3
    return jnp.concatenate(rows + [jnp.zeros((5, value.shape[1]), BF16)], axis=0)


def rows_by_rows(a, b):
    return lax.dot_general(a, b, (((0,), (0,)), ((), ())), preferred_element_type=F32)


def product(a, b):
    return lax.dot_general(a, b, (((1,), (0,)), ((), ())), preferred_element_type=F32)


def polynomial(z, terms):
    total = terms[-1]
    for term in terms[-2::-1]:
        total = term + z * total
    return total


def versine_and_sine(turns):
    g = turns - jnp.round(turns)
    s = g * polynomial(g * g, SINE)
    versine = s * s
    square = 2.0 - versine
    sine = s * (square * lax.rsqrt(square))
    return sine * sine, sine * (1.0 - versine)


def pipelined(tiles, phase, trig_weights, turns_ref, trig_ref, step):
    rows = turns_ref.shape[1]

    def elementwise(t):
        for r in range(0, rows, step):
            versine, sine = versine_and_sine(turns_ref[t % 2, r : r + step, :])
            for part, value in enumerate(halves(versine) + halves(sine)):
                trig_ref[t % 2, part, r : r + step, :] = value

    turns_ref[0] = phase(0)
    for t in range(tiles):
        if t + 1 < tiles:
            turns_ref[(t + 1) % 2] = phase(t + 1)
        if t > 0:
            trig_weights(t - 1)
        elementwise(t)
    trig_weights(tiles - 1)


def diagonal(width):
    shape = (8, width)
    return lax.broadcasted_iota(jnp.int32, shape, 0) == lax.broadcasted_iota(jnp.int32, shape, 1)


def structure_kernel(
    pos_hbm,
    load_hbm,
    dual_hbm,
    weight_hbm,
    slope_hbm,
    out_ref,
    own_atoms_ref,
    pos_ref,
    load_ref,
    dual_ref,
    weight_ref,
    slope_ref,
    p_ref,
    q_ref,
    w_ref,
    turns_ref,
    trig_ref,
    sems,
):
    pairs = (
        (dual_hbm, dual_ref),
        (pos_hbm, pos_ref),
        (load_hbm, load_ref),
        (weight_hbm, weight_ref),
        (slope_hbm, slope_ref),
    )
    copies = [
        pltpu.make_async_copy(source, target, sems.at[n]) for n, (source, target) in enumerate(pairs)
    ]
    for copy in copies:
        copy.start()
    atoms, vectors = pos_ref.shape[1], dual_ref.shape[1]
    bm, bn = turns_ref.shape[1:]
    copies[0].wait()
    q_ref[...] = spread(dual_ref[...] * (0.5 / np.pi), False)
    copies[1].wait()
    p_ref[...] = spread(pos_ref[...] - CENTRE, True)
    copies[2].wait()
    load = load_ref[...]
    w_ref[...] = jnp.concatenate(halves(load), axis=0)
    total = jnp.sum(load, axis=1, keepdims=True)
    tiles = [(i, j) for j in range(vectors // bn) for i in range(atoms // bm)]
    sums = {}

    def phase(t):
        i, j = tiles[t]
        return rows_by_rows(p_ref[:, i * bm : (i + 1) * bm], q_ref[:, j * bn : (j + 1) * bn])

    def weigh(t):
        i, j = tiles[t]
        w = w_ref[:, i * bm : (i + 1) * bm]
        for part in range(4):
            term = product(w, trig_ref[t % 2, part])
            sums[part // 2] = sums[part // 2] + term if part % 2 or i > 0 else term
        if i == atoms // bm - 1:
            real = total - 2.0 * (sums[0][:8] + sums[0][8:])
            imag = 2.0 * (sums[1][:8] + sums[1][8:])
            factors = jnp.concatenate([real, imag], axis=0)
            for lane in range(0, bn, 128):
                group = (j * bn + lane) // 128
                for row in range(16):
                    put(group, row // 4, row % 4, factors[row : row + 1, lane : lane + 128])

    def put(group, part, row, value):
        place = PLANE_ORDER.index((group % 4) * 8 + part * 2 + group // 4)
        out_ref[place, :, row * 128 : (row + 1) * 128] = value

    pipelined(len(tiles), phase, weigh, turns_ref, trig_ref, 16)

    copies[3].wait()
    for group in range(vectors // 128):
        lanes = slice(group * 128, (group + 1) * 128)
        for part in range(3):
            put(group, part, 4, dual_ref[part : part + 1, lanes])
        put(group, 3, 4, weight_ref[:, lanes])
    copies[4].wait()
    owned = own_atoms_ref.shape[1]
    mine = pl.ds(pl.multiple_of(lax.axis_index("k") * owned, 128), owned)
    own_atoms_ref[:8] = load_ref[:, mine]
    slope = jnp.concatenate([slope_ref[...], jnp.zeros((1, owned - 8), F32)], axis=1)
    own_atoms_ref[8:12] = jnp.concatenate([pos_ref[:, mine], slope], axis=0)


def structure(pos, load, dual, weights, slope, owned):
    atoms, vectors = pos.shape[1], dual.shape[1]
    bm, bn = 512, 256
    return pl.pallas_call(
        structure_kernel,
        out_shape=(
            pltpu.VMEM((32, 1, 640), F32),
            pltpu.VMEM((12, owned), F32),
        ),
        in_specs=[pl.BlockSpec(memory_space=pl.ANY)] * 5,
        out_specs=(pl.BlockSpec(memory_space=pltpu.VMEM),) * 2,
        scratch_shapes=[
            pltpu.VMEM(pos.shape, F32),
            pltpu.VMEM(load.shape, F32),
            pltpu.VMEM(dual.shape, F32),
            pltpu.VMEM(weights.shape, F32),
            pltpu.VMEM(slope.shape, F32),
            pltpu.VMEM((32, atoms), BF16),
            pltpu.VMEM((32, vectors), BF16),
            pltpu.VMEM((16, atoms), BF16),
            pltpu.VMEM((2, bm, bn), F32),
            pltpu.VMEM((2, 4, bm, bn), BF16),
            pltpu.SemaphoreType.DMA((5,)),
        ],
        compiler_params=pltpu.CompilerParams(vmem_limit_bytes=60 * 2**20),
        name="structure",
    )(pos, load, dual, weights, slope)


def spread_four(value, outer):
    twice = jnp.concatenate([value, value], axis=0)
    a = twice.astype(BF16).astype(F32)
    rest = twice - a
    b = rest.astype(BF16).astype(F32)
    c = rest - b
    first = lax.broadcasted_iota(jnp.int32, twice.shape, 0) < 4
    if outer:
        rows = [a, jnp.where(first, a, b), b, c]
    else:
        rows = [jnp.where(first, a, b), jnp.where(first, c, a), jnp.where(first, b, c), jnp.where(first, a, b)]
    return jnp.concatenate(rows, axis=0).astype(BF16)


def gradient_kernel(
    table_ref,
    atoms_ref,
    out_ref,
    p_ref,
    versine_ref,
    sine_ref,
    turns_ref,
    trig_ref,
    *,
    all_atoms,
):
    bm, owned = turns_ref.shape[1:]
    vectors = p_ref.shape[1]
    atoms = jnp.concatenate([atoms_ref[0], atoms_ref[1]], axis=1)
    load = atoms[:8]
    pos = jnp.concatenate([atoms[8:11] - CENTRE, jnp.zeros((1, owned), F32)], axis=0)
    q = spread_four(pos, False)
    slope = 4.0 * jnp.sum(jnp.where(diagonal(128), atoms_ref[0, 11:12, :128], 0.0), axis=1, keepdims=True)
    is_dual = lax.broadcasted_iota(jnp.int32, (4, 128), 0) < 3
    sums = {
        "energy": jnp.zeros((8, 128), F32),
        "constant": jnp.zeros((32, 128), F32),
        "high": jnp.zeros((64, owned), F32),
        "low": jnp.zeros((32, owned), F32),
    }

    def duals(b):
        places = [CORE_PLANE_ORDER.index((b // 8) * 4 + part) for part in range(4)]
        return jnp.concatenate([table_ref[pl.ds(at * 40 + 32 + b % 8, 1), :] for at in places], axis=0)

    def weights(b):
        g, zl = b // 8, b % 8
        rows = [
            table_ref[pl.ds(CORE_PLANE_ORDER.index(g * 4 + part) * 40 + zl, 4, stride=8), :]
            for part in range(4)
        ]
        dual = duals(b)
        real = jnp.concatenate(rows[:2], axis=0)
        imag = jnp.concatenate(rows[2:], axis=0)
        weight = dual[3:4]
        real_term, imag_term = weight * real, weight * imag
        sums["energy"] = sums["energy"] + (real_term * real + imag_term * imag)
        real_term, imag_term = slope * real_term, slope * imag_term
        at_versine = jnp.concatenate([-real_term] + [dual[d : d + 1] * imag_term for d in range(3)], axis=0)
        at_sine = jnp.concatenate([imag_term] + [dual[d : d + 1] * real_term for d in range(3)], axis=0)
        sums["constant"] = sums["constant"] + at_versine
        at = pl.ds(b * 128, 128)
        versine_ref[:, at] = jnp.concatenate(halves(at_versine), axis=0)
        sine_ref[:, at] = jnp.concatenate(halves(at_sine), axis=0)

    def phase(t):
        at = slice(t * bm, (t + 1) * bm)
        for b in range(t * bm // 128, (t + 1) * bm // 128):
            dual = jnp.where(is_dual, duals(b) * (0.5 / np.pi), 0.0)
            p_ref[:, b * 128 : (b + 1) * 128] = spread_four(dual, True)
        return rows_by_rows(p_ref[:, at], q)

    def weigh(t):
        at = slice(t * bm, (t + 1) * bm)
        for b in range(t * bm // 128, (t + 1) * bm // 128):
            weights(b)
        for part, ref in enumerate((versine_ref, sine_ref)):
            sums["high"] = sums["high"] + product(ref[:, at], trig_ref[t % 2, 2 * part])
            sums["low"] = sums["low"] + product(ref[:32, at], trig_ref[t % 2, 2 * part + 1])

    pipelined(vectors // bm, phase, weigh, turns_ref, trig_ref, 16)
    energy = jnp.sum(sums["energy"], axis=1, keepdims=True) * (1.0 / all_atoms)
    out = sums["high"][:32] + sums["high"][32:] + sums["low"]
    out = out - 0.5 * jnp.sum(sums["constant"], axis=1, keepdims=True)
    out_ref[:8] = out[:8]
    out_ref[8:12] = jnp.concatenate(
        [jnp.sum(load * out[8 * d + 8 : 8 * d + 16], axis=0, keepdims=True) for d in range(3)]
        + [jnp.sum(jnp.where(diagonal(owned), energy, 0.0), axis=0, keepdims=True)],
        axis=0,
    )


def gradients(table, atoms, vectors, all_atoms):
    owned = 2 * atoms.shape[2]
    bm = 256
    return pl.pallas_call(
        functools.partial(gradient_kernel, all_atoms=all_atoms),
        out_shape=pltpu.VMEM((12, owned), F32),
        in_specs=[pl.BlockSpec(memory_space=pltpu.VMEM)] * 2,
        out_specs=pl.BlockSpec(memory_space=pltpu.VMEM),
        scratch_shapes=[
            pltpu.VMEM((32, vectors), BF16),
            pltpu.VMEM((64, vectors), BF16),
            pltpu.VMEM((64, vectors), BF16),
            pltpu.VMEM((2, bm, owned), F32),
            pltpu.VMEM((2, 4, bm, owned), BF16),
        ],
        compiler_params=pltpu.CompilerParams(vmem_limit_bytes=40 * 2**20),
        name="gradients",
    )(table, atoms)


def finish_kernel(shares_ref, grad_ref, force_ref, energy_ref):
    owned = grad_ref.shape[1]
    mine = pl.ds(pl.multiple_of(lax.axis_index("c") * owned, 128), owned)
    grad_ref[...] = shares_ref[0, :8, mine] + shares_ref[1, :8, mine]
    force_ref[...] = shares_ref[0, 8:11, mine] + shares_ref[1, 8:11, mine]
    energy_ref[...] = shares_ref[0, 11:12, :8] + shares_ref[1, 11:12, :8]


def finish(shares):
    owned = shares.shape[2] // 2
    return pl.pallas_call(
        finish_kernel,
        out_shape=(
            jax.ShapeDtypeStruct((8, owned), F32),
            jax.ShapeDtypeStruct((3, owned), F32),
            jax.ShapeDtypeStruct((1, 8), F32),
        ),
        in_specs=[pl.BlockSpec(memory_space=pltpu.VMEM)],
        out_specs=(pl.BlockSpec(memory_space=pltpu.VMEM),) * 3,
        name="finish",
    )(shares)


def shards(pos, load, dual, weights, slope):
    owned = pos.shape[1] // lax.axis_size("k")
    partial, atoms = structure(
        pos, load, dual, weights.reshape(1, -1), slope.reshape(1, -1), owned
    )
    parts = lax.all_to_all(
        partial,
        PLANE,
        0,
        0,
        axis_index_groups=[PLANE_ORDER],
        tiled=True,
    )
    block = jnp.concatenate([jnp.sum(parts[:, :, :512], axis=0), parts[0, :, 512:]], axis=1)
    atoms, block = lax.optimization_barrier((atoms, block))
    atoms = lax.all_gather(atoms, "c")
    column = lax.all_to_all(
        jnp.broadcast_to(block, (16, 1, 640)),
        COLUMN,
        0,
        0,
        axis_index_groups=[list(COLUMN_ORDER)],
        tiled=True,
    )
    atoms, column = lax.optimization_barrier((atoms, column))
    column = column.reshape(2, 8, 5, 128)
    block = jnp.concatenate([column[1, :, :4] + column[0, :, :4], column[0, :, 4:]], axis=1)
    block = jnp.transpose(block, (1, 0, 2)).reshape(40, 128)
    table = lax.all_to_all(
        jnp.broadcast_to(block, (16, 40, 128)),
        ("x", "y"),
        0,
        0,
        axis_index_groups=[CORE_PLANE_ORDER],
        tiled=True,
    )
    vectors = dual.shape[1] * lax.axis_size("k") // 2
    all_atoms = pos.shape[1] * lax.axis_size(("zh",) + PLANE)
    shares = lax.all_gather(gradients(table.reshape(640, 128), atoms, vectors, all_atoms), "c")
    grad, force, energy = finish(shares)
    return grad, force, energy.reshape(8)


def solution(mesh):
    fine = Mesh(np.asarray(mesh.devices).reshape(2, 4, 4, 2, 8), ("zh",) + PLANE + ("k",))
    atom = ("zh",) + PLANE
    return jax.shard_map(
        shards,
        mesh=fine,
        in_specs=(P(None, atom), P(None, atom), P(None, "k"), P("k"), P()),
        out_specs=(P(None, atom + ("k",)), P(None, atom + ("k",)), P()),
        check_vma=False,
    )
```

```python
import functools

import jax
import jax.numpy as jnp
import numpy as np
from jax import lax
from jax.experimental import pallas as pl
from jax.experimental.pallas import tpu as pltpu
from jax.sharding import Mesh
from jax.sharding import PartitionSpec as P

BF16 = jnp.bfloat16
F32 = jnp.float32
PLANE = ("x", "y", "c")
COLUMN = ("zh", "k")
PLANE_ORDER = sorted(range(32), key=lambda p: (abs(p // 8 - 2) + abs(p // 2 % 4 - 2), p ^ 1))
CORE_PLANE_ORDER = sorted(range(16), key=lambda p: abs(p // 4 - 2) + abs(p % 4 - 2))
COLUMN_ORDER = (*range(8, 16), *range(8))
CENTRE = 70.0
SINE = (2.2214303016662598, -0.9131746292114258, 0.10983827710151672)


def halves(value):
    high = value.astype(BF16)
    return high, (value - high.astype(F32)).astype(BF16)


def pieces(value):
    first = value.astype(BF16)
    rest = value - first.astype(F32)
    second = rest.astype(BF16)
    return first, second, (rest - second.astype(F32)).astype(BF16)


def spread(value, outer):
    a, b, c = pieces(value)
    rows = [a, a, a, b, b, b, c, c, c] if outer else [a, b, c] * 3
    return jnp.concatenate(rows + [jnp.zeros((5, value.shape[1]), BF16)], axis=0)


def rows_by_rows(a, b):
    return lax.dot_general(a, b, (((0,), (0,)), ((), ())), preferred_element_type=F32)


def product(a, b):
    return lax.dot_general(a, b, (((1,), (0,)), ((), ())), preferred_element_type=F32)


def polynomial(z, terms):
    total = terms[-1]
    for term in terms[-2::-1]:
        total = term + z * total
    return total


def versine_and_sine(turns):
    g = turns - jnp.round(turns)
    s = g * polynomial(g * g, SINE)
    versine = s * s
    square = 2.0 - versine
    sine = s * (square * lax.rsqrt(square))
    return sine * sine, sine * (1.0 - versine)


def pipelined(tiles, phase, trig_weights, turns_ref, trig_ref, step):
    rows = turns_ref.shape[1]

    def elementwise(t):
        for r in range(0, rows, step):
            versine, sine = versine_and_sine(turns_ref[t % 2, r : r + step, :])
            for part, value in enumerate(halves(versine) + halves(sine)):
                trig_ref[t % 2, part, r : r + step, :] = value

    turns_ref[0] = phase(0)
    for t in range(tiles):
        if t + 1 < tiles:
            turns_ref[(t + 1) % 2] = phase(t + 1)
        if t > 0:
            trig_weights(t - 1)
        elementwise(t)
    trig_weights(tiles - 1)


def diagonal(width):
    shape = (8, width)
    return lax.broadcasted_iota(jnp.int32, shape, 0) == lax.broadcasted_iota(jnp.int32, shape, 1)


def structure_kernel(
    pos_hbm,
    load_hbm,
    dual_hbm,
    weight_hbm,
    slope_hbm,
    out_ref,
    own_atoms_ref,
    pos_ref,
    load_ref,
    dual_ref,
    weight_ref,
    slope_ref,
    p_ref,
    q_ref,
    w_ref,
    turns_ref,
    trig_ref,
    sems,
):
    pairs = (
        (dual_hbm, dual_ref),
        (pos_hbm, pos_ref),
        (load_hbm, load_ref),
        (weight_hbm, weight_ref),
        (slope_hbm, slope_ref),
    )
    copies = [
        pltpu.make_async_copy(source, target, sems.at[n]) for n, (source, target) in enumerate(pairs)
    ]
    for copy in copies:
        copy.start()
    atoms, vectors = pos_ref.shape[1], dual_ref.shape[1]
    bm, bn = turns_ref.shape[1:]
    copies[0].wait()
    q_ref[...] = spread(dual_ref[...] * (0.5 / np.pi), False)
    copies[1].wait()
    p_ref[...] = spread(pos_ref[...] - CENTRE, True)
    copies[2].wait()
    load = load_ref[...]
    w_ref[...] = jnp.concatenate(halves(load), axis=0)
    total = jnp.sum(load, axis=1, keepdims=True)
    tiles = [(i, j) for j in range(vectors // bn) for i in range(atoms // bm)]
    sums = {}

    def phase(t):
        i, j = tiles[t]
        return rows_by_rows(p_ref[:, i * bm : (i + 1) * bm], q_ref[:, j * bn : (j + 1) * bn])

    def weigh(t):
        i, j = tiles[t]
        if t == 1:
            hand_out()
        w = w_ref[:, i * bm : (i + 1) * bm]
        for part in range(4):
            term = product(w, trig_ref[t % 2, part])
            sums[part // 2] = sums[part // 2] + term if part % 2 or i > 0 else term
        if i == atoms // bm - 1:
            real = total - 2.0 * (sums[0][:8] + sums[0][8:])
            imag = 2.0 * (sums[1][:8] + sums[1][8:])
            factors = jnp.concatenate([real, imag], axis=0)
            for lane in range(0, bn, 128):
                group = (j * bn + lane) // 128
                for row in range(16):
                    put(group, row // 4, row % 4, factors[row : row + 1, lane : lane + 128])

    def put(group, part, row, value):
        place = PLANE_ORDER.index((group % 4) * 8 + part * 2 + group // 4)
        out_ref[place, :, row * 128 : (row + 1) * 128] = value

    def hand_out():
        copies[3].wait()
        for group in range(vectors // 128):
            lanes = slice(group * 128, (group + 1) * 128)
            for part in range(3):
                put(group, part, 4, dual_ref[part : part + 1, lanes])
            put(group, 3, 4, weight_ref[:, lanes])
        copies[4].wait()
        owned = own_atoms_ref.shape[1]
        mine = pl.ds(pl.multiple_of(lax.axis_index("k") * owned, 128), owned)
        own_atoms_ref[:8] = load_ref[:, mine]
        slope = jnp.concatenate([slope_ref[...], jnp.zeros((1, owned - 8), F32)], axis=1)
        own_atoms_ref[8:12] = jnp.concatenate([pos_ref[:, mine], slope], axis=0)

    pipelined(len(tiles), phase, weigh, turns_ref, trig_ref, 16)


def structure(pos, load, dual, weights, slope, owned):
    atoms, vectors = pos.shape[1], dual.shape[1]
    bm, bn = 512, 256
    return pl.pallas_call(
        structure_kernel,
        out_shape=(
            pltpu.VMEM((32, 1, 640), F32),
            pltpu.VMEM((12, owned), F32),
        ),
        in_specs=[pl.BlockSpec(memory_space=pl.ANY)] * 5,
        out_specs=(pl.BlockSpec(memory_space=pltpu.VMEM),) * 2,
        scratch_shapes=[
            pltpu.VMEM(pos.shape, F32),
            pltpu.VMEM(load.shape, F32),
            pltpu.VMEM(dual.shape, F32),
            pltpu.VMEM(weights.shape, F32),
            pltpu.VMEM(slope.shape, F32),
            pltpu.VMEM((32, atoms), BF16),
            pltpu.VMEM((32, vectors), BF16),
            pltpu.VMEM((16, atoms), BF16),
            pltpu.VMEM((2, bm, bn), F32),
            pltpu.VMEM((2, 4, bm, bn), BF16),
            pltpu.SemaphoreType.DMA((5,)),
        ],
        compiler_params=pltpu.CompilerParams(vmem_limit_bytes=60 * 2**20),
        name="structure",
    )(pos, load, dual, weights, slope)


def spread_four(value, outer):
    twice = jnp.concatenate([value, value], axis=0)
    a = twice.astype(BF16).astype(F32)
    rest = twice - a
    b = rest.astype(BF16).astype(F32)
    c = rest - b
    first = lax.broadcasted_iota(jnp.int32, twice.shape, 0) < 4
    if outer:
        rows = [a, jnp.where(first, a, b), b, c]
    else:
        rows = [jnp.where(first, a, b), jnp.where(first, c, a), jnp.where(first, b, c), jnp.where(first, a, b)]
    return jnp.concatenate(rows, axis=0).astype(BF16)


def gradient_kernel(
    table_ref,
    atoms_ref,
    out_ref,
    p_ref,
    versine_ref,
    sine_ref,
    turns_ref,
    trig_ref,
    *,
    all_atoms,
):
    bm, owned = turns_ref.shape[1:]
    vectors = p_ref.shape[1]
    atoms = jnp.concatenate([atoms_ref[0], atoms_ref[1]], axis=1)
    load = atoms[:8]
    pos = jnp.concatenate([atoms[8:11] - CENTRE, jnp.zeros((1, owned), F32)], axis=0)
    q = spread_four(pos, False)
    slope = 4.0 * jnp.sum(jnp.where(diagonal(128), atoms_ref[0, 11:12, :128], 0.0), axis=1, keepdims=True)
    is_dual = lax.broadcasted_iota(jnp.int32, (4, 128), 0) < 3
    sums = {
        "energy": jnp.zeros((8, 128), F32),
        "constant": jnp.zeros((32, 128), F32),
        "high": jnp.zeros((64, owned), F32),
        "low": jnp.zeros((32, owned), F32),
    }

    def duals(b):
        places = [CORE_PLANE_ORDER.index((b // 8) * 4 + part) for part in range(4)]
        return jnp.concatenate([table_ref[pl.ds(at * 40 + 32 + b % 8, 1), :] for at in places], axis=0)

    def weights(b):
        g, zl = b // 8, b % 8
        rows = [
            table_ref[pl.ds(CORE_PLANE_ORDER.index(g * 4 + part) * 40 + zl, 4, stride=8), :]
            for part in range(4)
        ]
        dual = duals(b)
        real = jnp.concatenate(rows[:2], axis=0)
        imag = jnp.concatenate(rows[2:], axis=0)
        weight = dual[3:4]
        real_term, imag_term = weight * real, weight * imag
        sums["energy"] = sums["energy"] + (real_term * real + imag_term * imag)
        real_term, imag_term = slope * real_term, slope * imag_term
        at_versine = jnp.concatenate([-real_term] + [dual[d : d + 1] * imag_term for d in range(3)], axis=0)
        at_sine = jnp.concatenate([imag_term] + [dual[d : d + 1] * real_term for d in range(3)], axis=0)
        sums["constant"] = sums["constant"] + at_versine
        at = pl.ds(b * 128, 128)
        versine_ref[:, at] = jnp.concatenate(halves(at_versine), axis=0)
        sine_ref[:, at] = jnp.concatenate(halves(at_sine), axis=0)

    def phase(t):
        at = slice(t * bm, (t + 1) * bm)
        for b in range(t * bm // 128, (t + 1) * bm // 128):
            dual = jnp.where(is_dual, duals(b) * (0.5 / np.pi), 0.0)
            p_ref[:, b * 128 : (b + 1) * 128] = spread_four(dual, True)
        return rows_by_rows(p_ref[:, at], q)

    def weigh(t):
        at = slice(t * bm, (t + 1) * bm)
        for b in range(t * bm // 128, (t + 1) * bm // 128):
            weights(b)
        for part, ref in enumerate((versine_ref, sine_ref)):
            sums["high"] = sums["high"] + product(ref[:, at], trig_ref[t % 2, 2 * part])
            sums["low"] = sums["low"] + product(ref[:32, at], trig_ref[t % 2, 2 * part + 1])

    pipelined(vectors // bm, phase, weigh, turns_ref, trig_ref, 16)
    energy = jnp.sum(sums["energy"], axis=1, keepdims=True) * (1.0 / all_atoms)
    out = sums["high"][:32] + sums["high"][32:] + sums["low"]
    out = out - 0.5 * jnp.sum(sums["constant"], axis=1, keepdims=True)
    out_ref[:8] = out[:8]
    out_ref[8:12] = jnp.concatenate(
        [jnp.sum(load * out[8 * d + 8 : 8 * d + 16], axis=0, keepdims=True) for d in range(3)]
        + [jnp.sum(jnp.where(diagonal(owned), energy, 0.0), axis=0, keepdims=True)],
        axis=0,
    )


def gradients(table, atoms, vectors, all_atoms):
    owned = 2 * atoms.shape[2]
    bm = 256
    return pl.pallas_call(
        functools.partial(gradient_kernel, all_atoms=all_atoms),
        out_shape=pltpu.VMEM((12, owned), F32),
        in_specs=[pl.BlockSpec(memory_space=pltpu.VMEM)] * 2,
        out_specs=pl.BlockSpec(memory_space=pltpu.VMEM),
        scratch_shapes=[
            pltpu.VMEM((32, vectors), BF16),
            pltpu.VMEM((64, vectors), BF16),
            pltpu.VMEM((64, vectors), BF16),
            pltpu.VMEM((2, bm, owned), F32),
            pltpu.VMEM((2, 4, bm, owned), BF16),
        ],
        compiler_params=pltpu.CompilerParams(vmem_limit_bytes=40 * 2**20),
        name="gradients",
    )(table, atoms)


def finish_kernel(shares_ref, grad_ref, force_ref, energy_ref):
    owned = grad_ref.shape[1]
    mine = pl.ds(pl.multiple_of(lax.axis_index("c") * owned, 128), owned)
    grad_ref[...] = shares_ref[0, :8, mine] + shares_ref[1, :8, mine]
    force_ref[...] = shares_ref[0, 8:11, mine] + shares_ref[1, 8:11, mine]
    energy_ref[...] = shares_ref[0, 11:12, :8] + shares_ref[1, 11:12, :8]


def finish(shares):
    owned = shares.shape[2] // 2
    return pl.pallas_call(
        finish_kernel,
        out_shape=(
            jax.ShapeDtypeStruct((8, owned), F32),
            jax.ShapeDtypeStruct((3, owned), F32),
            jax.ShapeDtypeStruct((1, 8), F32),
        ),
        in_specs=[pl.BlockSpec(memory_space=pltpu.VMEM)],
        out_specs=(pl.BlockSpec(memory_space=pltpu.VMEM),) * 3,
        name="finish",
    )(shares)


def shards(pos, load, dual, weights, slope):
    owned = pos.shape[1] // lax.axis_size("k")
    partial, atoms = structure(
        pos, load, dual, weights.reshape(1, -1), slope.reshape(1, -1), owned
    )
    parts = lax.all_to_all(
        partial,
        PLANE,
        0,
        0,
        axis_index_groups=[PLANE_ORDER],
        tiled=True,
    )
    block = jnp.concatenate([jnp.sum(parts[:, :, :512], axis=0), parts[0, :, 512:]], axis=1)
    atoms, block = lax.optimization_barrier((atoms, block))
    atoms = lax.all_gather(atoms, "c")
    column = lax.all_to_all(
        jnp.broadcast_to(block, (16, 1, 640)),
        COLUMN,
        0,
        0,
        axis_index_groups=[list(COLUMN_ORDER)],
        tiled=True,
    )
    atoms, column = lax.optimization_barrier((atoms, column))
    column = column.reshape(2, 8, 5, 128)
    block = jnp.concatenate([column[1, :, :4] + column[0, :, :4], column[0, :, 4:]], axis=1)
    block = jnp.transpose(block, (1, 0, 2)).reshape(40, 128)
    table = lax.all_to_all(
        jnp.broadcast_to(block, (16, 40, 128)),
        ("x", "y"),
        0,
        0,
        axis_index_groups=[CORE_PLANE_ORDER],
        tiled=True,
    )
    vectors = dual.shape[1] * lax.axis_size("k") // 2
    all_atoms = pos.shape[1] * lax.axis_size(("zh",) + PLANE)
    shares = lax.all_gather(gradients(table.reshape(640, 128), atoms, vectors, all_atoms), "c")
    grad, force, energy = finish(shares)
    return grad, force, energy.reshape(8)


def solution(mesh):
    fine = Mesh(np.asarray(mesh.devices).reshape(2, 4, 4, 2, 8), ("zh",) + PLANE + ("k",))
    atom = ("zh",) + PLANE
    return jax.shard_map(
        shards,
        mesh=fine,
        in_specs=(P(None, atom), P(None, atom), P(None, "k"), P("k"), P()),
        out_specs=(P(None, atom + ("k",)), P(None, atom + ("k",)), P()),
        check_vma=False,
    )
```
